32 devices in a mesh: dp: 8 (over z, x), mp: 4 (over y, core).
Axes of the slice: x: 2, y: 2, z: 4, core: 2. Of those that a mesh axis runs over, the one named last changes fastest.
Arguments:
- tokens: bfloat16 [1024, 16384], P('dp', 'mp'), may hold values from -6 to 6
- cotangent: bfloat16 [1024, 16384], P('dp', 'mp'), may hold values from -6 to 6
- right_one: bfloat16 [128, 128, 128], P('mp', 'dp'), may hold values from -0.5 to 0.5
- left_one: bfloat16 [128, 128, 128], P('mp', 'dp'), may hold values from -0.5 to 0.5
- right_two: bfloat16 [128, 128, 128], P('mp', 'dp'), may hold values from -0.5 to 0.5
- left_two: bfloat16 [128, 128, 128], P('mp', 'dp'), may hold values from -0.5 to 0.5
Outputs:
- tokens_grad: bfloat16 [1024, 16384], P('dp', 'mp')
- right_one_grad: float32 [128, 128, 128], P('mp', 'dp')
- left_one_grad: float32 [128, 128, 128], P('mp', 'dp')
- right_two_grad: float32 [128, 128, 128], P('mp', 'dp')
- left_two_grad: float32 [128, 128, 128], P('mp', 'dp')
The draws below stay inside these ranges and needn't reach their ends.
All inputs are finite; a program needn't handle non-finite values.
Results may differ from the reference program's by a relative error of at most 0.0072.
Values may be sent and summed in bfloat16 or wider, within the bound.
No kernel may reach another device: no remote copies, remote signals or barrier semaphores. Data moves between devices by JAX's collectives and lax.ppermute only.
A program may use at most 64 MiB of HBM per device.

```python
import math
import jax
import jax.numpy as jnp
from jax import lax

NB = 128
BS = 128
D = 16384
TOK_DEV = 128
TOKENS = 1024
N_DP = 8


def shard_levels(key, extent, cuts, smallest, high):
    def one(dim, blocks):
        steps = jax.random.uniform(jax.random.fold_in(jax.random.fold_in(key, 6), dim), (blocks,), jnp.float32, smallest / len(cuts), high / len(cuts))
        return jnp.repeat(jnp.exp(steps), extent[dim] // blocks).reshape((-1,) + (1,) * (len(extent) - dim - 1))

    loudness = one(*cuts[0])
    for cut in cuts[1:]:
        loudness = loudness * one(*cut)
    return loudness


def normal_values(stream_key, dims, scale, reach, pieces=(), held_as=jnp.bfloat16):
    loudness = shard_levels(stream_key, dims, pieces, -0.22, 0.18) if pieces else 1.0
    drawn = jax.random.normal(stream_key, dims, jnp.float32) * scale * loudness
    return jnp.minimum(jnp.maximum(drawn, -reach), reach).astype(held_as)


def setup_inputs(seed: int = 0) -> dict:
    seeds = jax.random.split(jax.random.key(seed), 7)
    tokens = normal_values(seeds[0], (TOKENS, D), 1.0, 6.0, ((0, 8), (1, 4)))
    cotangent = normal_values(seeds[1], (TOKENS, D), 1.0, 6.0, ((0, 8), (1, 4)))
    right_one = normal_values(seeds[2], (NB, BS, BS), BS ** -0.5, 0.5, ((0, 4), (1, 8)))
    left_one = normal_values(seeds[3], (NB, BS, BS), NB ** -0.5, 0.5, ((0, 4), (1, 8)))
    right_two = normal_values(seeds[4], (NB, BS, BS), BS ** -0.5, 0.5, ((0, 4), (1, 8)))
    left_two = normal_values(seeds[5], (NB, BS, BS), NB ** -0.5, 0.5, ((0, 4), (1, 8)))
    return dict(tokens=tokens, cotangent=cotangent, right_one=right_one, left_one=left_one, right_two=right_two, left_two=left_two)


half_root = 0.7071067811865476
inv_root_tau = 0.3989422804014327

def gelu_parts(values):
    normal_cdf = 0.5 * (1.0 + lax.erf(values * half_root))
    return (values * normal_cdf, normal_cdf + values * jnp.exp(-0.5 * values * values) * inv_root_tau)

def widen(array):
    return array.astype(jnp.float32)

def reference(tokens, cotangent, right_one, left_one, right_two, left_two):
    inputs = tokens.reshape(N_DP, TOK_DEV, NB, BS)
    upstream = cotangent.reshape(N_DP, TOK_DEV, NB, BS)
    right_first = widen(right_one)
    left_first = widen(left_one)
    right_second = widen(right_two)
    left_second = widen(left_two)

    def one_block(totals, pair):
        block_in, block_cot = pair
        wide_in = widen(block_in)
        wide_cot = widen(block_cot)
        first_mixed = jnp.einsum('tbi,bij->tbj', wide_in, right_first).astype(jnp.bfloat16)
        preact = jnp.einsum('tbj,jbk->tkj', widen(first_mixed), left_first).astype(jnp.bfloat16)
        activated, slope = gelu_parts(widen(preact))
        hidden = activated.astype(jnp.bfloat16)
        second_mixed = jnp.einsum('tbi,bij->tbj', widen(hidden), right_second).astype(jnp.bfloat16)
        grad_left_two = jnp.einsum('tbj,tkj->jbk', widen(second_mixed), wide_cot)
        second_back = jnp.einsum('tkj,jbk->tbj', wide_cot, left_second).astype(jnp.bfloat16)
        grad_right_two = jnp.einsum('tbi,tbj->bij', widen(hidden), widen(second_back))
        back_hidden = jnp.einsum('tbj,bij->tbi', widen(second_back), right_second)
        grad_preact = (back_hidden * slope).astype(jnp.bfloat16)
        grad_left_one = jnp.einsum('tbj,tkj->jbk', widen(first_mixed), widen(grad_preact))
        first_back = jnp.einsum('tkj,jbk->tbj', widen(grad_preact), left_first).astype(jnp.bfloat16)
        grad_right_one = jnp.einsum('tbi,tbj->bij', wide_in, widen(first_back))
        grad_tokens = jnp.einsum('tbj,bij->tbi', widen(first_back), right_first).astype(jnp.bfloat16)
        updated = (totals[0] + grad_right_one, totals[1] + grad_left_one, totals[2] + grad_right_two, totals[3] + grad_left_two)
        return (updated, grad_tokens)
    zeros = jnp.zeros((NB, BS, BS), jnp.float32)
    totals, grads = lax.scan(one_block, (zeros, zeros, zeros, zeros), (inputs, upstream))
    scale = 1.0 / math.sqrt(TOKENS)
    return (grads.reshape(TOKENS, D), totals[0] * scale, totals[1] * scale, totals[2] * scale, totals[3] * scale)
```

```python
import math

import jax
import jax.numpy as jnp
from jax import lax
from jax.sharding import PartitionSpec as P

half_root = 0.7071067811865476
inv_root_tau = 0.3989422804014327


def gelu_parts(values):
    normal_cdf = 0.5 * (1.0 + lax.erf(values * half_root))
    return (
        values * normal_cdf,
        normal_cdf + values * jnp.exp(-0.5 * values * values) * inv_root_tau,
    )


def to_blocks(source):
    return lax.all_to_all(source, "mp", split_axis=0, concat_axis=1, tiled=True)


def to_rows(source):
    return lax.all_to_all(source, "mp", split_axis=1, concat_axis=0, tiled=True)


def grad_columns(source, left_full):
    received = lax.all_to_all(source, "mp", split_axis=0, concat_axis=1, tiled=True)
    passed = jnp.einsum(
        "jkt,jbk->jbt", received, left_full, preferred_element_type=jnp.float32
    ).astype(jnp.bfloat16)
    return (received, passed)


def hop(source, axis, offset):
    size = lax.axis_size(axis)
    return lax.ppermute(source, axis, [(i, i ^ offset) for i in range(size)])


def reorder(pieces):
    size = pieces.shape[0]
    me = lax.axis_index("dp")
    bits = size.bit_length() - 1
    rest = pieces.shape[1:]
    pieces = pieces.reshape((2,) * bits + rest)
    for bit in range(bits):
        axis = bits - 1 - bit
        pieces = jnp.where((me >> bit) & 1 == 1, jnp.flip(pieces, axis), pieces)
    return pieces.reshape((size,) + rest)


def gather_rows(shard):
    size = lax.axis_size("dp")
    held = jnp.stack([shard] + [hop(shard, "dp", r) for r in range(2, size, 2)])
    other = hop(held, "dp", 1)
    pieces = jnp.stack([held, other], axis=1).reshape((size,) + shard.shape)
    blocks, rows, width = shard.shape
    return jnp.transpose(reorder(pieces), (1, 0, 2, 3)).reshape(blocks, size * rows, width)


def scatter_rows(grad, scale):
    size = lax.axis_size("dp")
    blocks, rows, width = grad.shape
    pieces = reorder(jnp.transpose(grad.reshape(blocks, size, rows // size, width), (1, 0, 2, 3)))
    pieces = pieces.reshape(size // 2, 2, blocks, rows // size, width)
    arrived = hop(pieces[:, 1].astype(jnp.bfloat16), "dp", 1)
    held = pieces[:, 0] + arrived.astype(jnp.float32)
    total = held[0]
    for q in range(1, size // 2):
        total = total + hop(held[q].astype(jnp.bfloat16), "dp", 2 * q).astype(jnp.float32)
    return total * scale


def on_device(tokens, cotangent, right_one, left_one, right_two, left_two):
    rows = tokens.shape[0]
    local_blocks = right_one.shape[0]
    block_size = right_one.shape[2]
    scale = 1.0 / math.sqrt(rows * lax.axis_size("dp"))
    inputs = tokens.reshape(rows, local_blocks, block_size)
    right_first, left_first, right_second, left_second = (
        gather_rows(right_one),
        gather_rows(left_one),
        gather_rows(right_two),
        gather_rows(left_two),
    )
    first_mixed = jnp.einsum(
        "tbi,bij->jbt", inputs, right_first, preferred_element_type=jnp.float32
    ).astype(jnp.bfloat16)
    first_columns = to_blocks(first_mixed)
    first_outer = jnp.einsum(
        "jbt,jbk->kjt", first_columns, left_first, preferred_element_type=jnp.float32
    ).astype(jnp.bfloat16)
    preact = to_blocks(first_outer)
    activated, slope = gelu_parts(preact.astype(jnp.float32))
    hidden = activated.astype(jnp.bfloat16)
    second_mixed = jnp.einsum(
        "bit,bij->jbt", hidden, right_second, preferred_element_type=jnp.float32
    ).astype(jnp.bfloat16)
    upstream = jnp.transpose(cotangent.reshape(rows, local_blocks, block_size), (2, 1, 0))
    second_columns = to_blocks(second_mixed)
    upstream_columns, second_back = grad_columns(upstream, left_second)
    grad_left_two = jnp.einsum(
        "jbt,jkt->jbk", second_columns, upstream_columns, preferred_element_type=jnp.float32
    )
    second_rows = to_rows(second_back)
    grad_right_two = jnp.einsum(
        "bit,jbt->bij", hidden, second_rows, preferred_element_type=jnp.float32
    )
    back_hidden = jnp.einsum(
        "jbt,bij->bit", second_rows, right_second, preferred_element_type=jnp.float32
    )
    grad_preact = jnp.transpose((back_hidden * slope).astype(jnp.bfloat16), (1, 0, 2))
    first_upstream, first_back = grad_columns(grad_preact, left_first)
    grad_left_one = jnp.einsum(
        "jbt,jkt->jbk", first_columns, first_upstream, preferred_element_type=jnp.float32
    )
    first_rows = to_rows(first_back)
    grad_right_one = jnp.einsum(
        "tbi,jbt->bij", inputs, first_rows, preferred_element_type=jnp.float32
    )
    tokens_grad = jnp.einsum(
        "jbt,bij->tbi", first_rows, right_first, preferred_element_type=jnp.float32
    ).astype(jnp.bfloat16)
    tokens_grad = tokens_grad.reshape(rows, local_blocks * block_size)
    summed = (
        scatter_rows(grad_right_one, scale),
        scatter_rows(grad_left_one, scale),
        scatter_rows(grad_right_two, scale),
        scatter_rows(grad_left_two, scale),
    )
    return (tokens_grad, summed[0], summed[1], summed[2], summed[3])


def solution(mesh):
    placed = (
        P("dp", "mp"),
        P("dp", "mp"),
        P("mp", "dp", None),
        P("mp", "dp", None),
        P("mp", "dp", None),
        P("mp", "dp", None),
    )
    return jax.shard_map(
        on_device,
        mesh=mesh,
        in_specs=placed,
        out_specs=(
            P("dp", "mp"),
            P("mp", "dp", None),
            P("mp", "dp", None),
            P("mp", "dp", None),
            P("mp", "dp", None),
        ),
        check_vma=False,
    )
```

```python
import functools
import math

import jax
import jax.numpy as jnp
from jax import lax
from jax.experimental import pallas as pl
from jax.experimental.pallas import tpu as pltpu
from jax.sharding import PartitionSpec as P

half_root = 0.7071067811865476
inv_root_tau = 0.3989422804014327
lane_tile = 128
packed_rows = 16
vmem_bytes = 56 * 1024 * 1024


def gelu_parts(values):
    normal_cdf = 0.5 * (1.0 + lax.erf(values * half_root))
    return (
        values * normal_cdf,
        normal_cdf + values * jnp.exp(-0.5 * values * values) * inv_root_tau,
    )


def hop(source, axis, offset):
    size = lax.axis_size(axis)
    return lax.ppermute(source, axis, [(i, i ^ offset) for i in range(size)])


def exchange(sends):
    return [sends[0]] + [hop(sends[q], "mp", q) for q in range(1, len(sends))]


def gather_rows(shard):
    size = lax.axis_size("dp")
    held = [shard] + [hop(shard, "dp", r) for r in range(2, size, 2)]
    other = [hop(piece, "dp", 1) for piece in held]
    pieces = [piece for pair in zip(held, other) for piece in pair]
    if shard.shape[1] % packed_rows == 0:
        return [piece.reshape(-1, shard.shape[2]) for piece in pieces]
    return [reorder(jnp.stack(pieces))]


def reorder(pieces):
    size, local, rows, width = pieces.shape
    me = lax.axis_index("dp")
    bits = size.bit_length() - 1
    pieces = pieces.reshape((2,) * bits + (local, rows, width))
    for bit in range(bits):
        axis = bits - 1 - bit
        pieces = jnp.where((me >> bit) & 1 == 1, jnp.flip(pieces, axis), pieces)
    pieces = jnp.transpose(pieces.reshape(size, local, rows, width), (1, 0, 2, 3))
    return pieces.reshape(local * size * rows, width)


def scatter_rows(sent, kept, scale):
    held = kept + hop(sent, "dp", 1).astype(jnp.float32)
    total = held[0]
    for q in range(1, held.shape[0]):
        total = total + hop(held[q].astype(jnp.bfloat16), "dp", 2 * q).astype(jnp.float32)
    return total * scale


class Sizes:
    def __init__(self, tokens, right_one):
        self.tokens = tokens.shape[0]
        self.local, self.rows, self.block = right_one.shape
        self.dp = lax.axis_size("dp")
        self.mp = lax.axis_size("mp")


def matmul(left, right, left_dim, right_dim):
    return lax.dot_general(
        left, right, (((left_dim,), (right_dim,)), ((), ())), preferred_element_type=jnp.float32
    )


def place(full, pieces, index):
    local, block, width = full.shape
    rows = block // len(pieces)
    if len(pieces) == 1:
        full[...] = pieces[0][...].reshape(local, rows, width)
        return
    for q, piece in enumerate(pieces):
        start = pl.multiple_of((index ^ q) * rows, rows)
        full[:, pl.ds(start, rows), :] = piece[...].reshape(local, rows, width)


def spread(mixed, sends, index):
    size = sends[0].shape[0]
    for q, send in enumerate(sends):
        start = pl.multiple_of((index ^ q) * size, size)
        for h in range(mixed.shape[0]):
            lanes = slice(h * lane_tile, (h + 1) * lane_tile)
            send[:, lanes] = mixed[h, pl.ds(start, size), :].astype(jnp.bfloat16)


def split_grad(sums, sent, kept, index):
    pairs = sent.shape[0]
    local, block, width = sums.shape
    rows = block // (2 * pairs)
    for q in range(pairs):
        for target, offset in ((kept, 2 * q), (sent, 2 * q + 1)):
            start = pl.multiple_of((index ^ offset) * rows, rows)
            part = sums[:, pl.ds(start, rows), :].reshape(local * rows, width)
            target[q] = part.astype(target.dtype)


def column(mixed, c, local, value):
    for h in range(mixed.shape[0]):
        lanes = slice(h * lane_tile, (h + 1) * lane_tile)
        mixed[h, pl.ds(c, value.shape[0], stride=local), :] = value[:, lanes]


def turn_kernel(z, ids, cotangent, *refs):
    sends, (mixed,) = refs[: z.mp], refs[z.mp :]
    for c in range(z.local):
        part = cotangent[:, c * z.block : (c + 1) * z.block].astype(jnp.float32)
        column(mixed, c, z.local, part.T)
    spread(mixed, sends, ids[1])


def first_kernel(z, count, ids, tokens, *refs):
    pieces, refs = refs[:count], refs[count:]
    full, sends, mixed = refs[0], refs[1 : 1 + z.mp], refs[1 + z.mp]
    place(full, pieces, ids[0])
    for c in range(z.local):
        part = tokens[:, c * z.block : (c + 1) * z.block]
        column(mixed, c, z.local, matmul(full[c], part, 0, 1))
    spread(mixed, sends, ids[1])


def middle_kernel(z, count, side, ids, *refs):
    pieces, arrived, refs = refs[:count], refs[count : count + z.mp], refs[count + z.mp :]
    full, columns, sends, mixed = refs[0], refs[1], refs[2 : 2 + z.mp], refs[2 + z.mp]
    place(full, pieces, ids[0])
    place(columns, arrived, ids[1])
    for c in range(z.local):
        column(mixed, c, z.local, matmul(full[c], columns[c], side, 0))
    spread(mixed, sends, ids[1])


def gelu_kernel(z, count, ids, *refs):
    pieces, refs = refs[:count], refs[count:]
    preact, backs, refs = refs[: z.mp], refs[z.mp : 2 * z.mp], refs[2 * z.mp :]
    full, hidden, back, sends, mixed = refs[0], refs[1], refs[2], refs[3 : 3 + z.mp], refs[3 + z.mp]
    place(full, pieces, ids[0])
    place(hidden, preact, ids[1])
    place(back, backs, ids[1])
    for c in range(z.local):
        activated, slope = gelu_parts(hidden[c].astype(jnp.float32))
        hidden[c] = activated.astype(jnp.bfloat16)
        column(mixed, c, z.local, matmul(full[c], back[c], 1, 0) * slope)
    spread(mixed, sends, ids[1])


def second_kernel(z, ids, full, hidden, *refs):
    sends, (mixed,) = refs[: z.mp], refs[z.mp :]
    for c in range(z.local):
        column(mixed, c, z.local, matmul(full[c], hidden[c], 0, 0))
    spread(mixed, sends, ids[1])


def grad_kernel(z, ids, left, right, sent, kept, sums):
    for c in range(z.local):
        sums[c] = matmul(left[c], right[c], 1, 1)
    split_grad(sums, sent, kept, ids[0])


def placed_grad_kernel(z, ids, right, *refs):
    pieces, (sent, kept, left, sums) = refs[: z.mp], refs[z.mp :]
    place(left, pieces, ids[1])
    grad_kernel(z, ids, left, right, sent, kept, sums)


def last_grad_kernel(z, ids, tokens, *refs):
    pieces, (turned, sent, kept, back, sums) = refs[: z.mp], refs[z.mp :]
    place(back, pieces, ids[1])
    for c in range(z.local):
        block = back[c].T
        turned[c] = block
        sums[c] = matmul(tokens[:, c * z.block : (c + 1) * z.block], block, 0, 0)
    split_grad(sums, sent, kept, ids[0])


def tokens_kernel(z, full, turned, out):
    for c in range(z.local):
        part = matmul(turned[c], full[c], 1, 1)
        out[:, c * z.block : (c + 1) * z.block] = part.astype(jnp.bfloat16)


def shaped(kind, *shape):
    return jax.ShapeDtypeStruct(shape, kind)


def run(body, outs, scratch, inputs, products):
    specs = [
        pl.BlockSpec(memory_space=pltpu.SMEM if one.dtype == jnp.int32 else pltpu.VMEM) for one in inputs
    ]
    moved = sum(math.prod(one.shape) * one.dtype.itemsize for one in (*inputs, *outs))
    return pl.pallas_call(
        body,
        out_shape=outs,
        in_specs=specs,
        out_specs=[pl.BlockSpec(memory_space=pltpu.VMEM) for _ in outs],
        scratch_shapes=scratch,
        compiler_params=pltpu.CompilerParams(vmem_limit_bytes=vmem_bytes),
        cost_estimate=pl.CostEstimate(flops=2 * products, bytes_accessed=moved, transcendentals=0),
    )(*inputs)


def on_device(tokens, cotangent, right_one, left_one, right_two, left_two):
    z = Sizes(tokens, right_one)
    bf16, f32 = jnp.bfloat16, jnp.float32
    scale = 1.0 / math.sqrt(z.tokens * z.dp)
    ids = jnp.stack([lax.axis_index("dp"), lax.axis_index("mp")]).astype(jnp.int32)
    products = z.local * z.block * z.block * z.tokens
    weight = shaped(bf16, z.local, z.block, z.block)
    acts = shaped(bf16, z.local, z.block, z.tokens)
    sends = [shaped(bf16, z.local * z.local, z.tokens)] * z.mp
    halves = [
        shaped(bf16, z.dp // 2, z.local * z.rows, z.block),
        shaped(f32, z.dp // 2, z.local * z.rows, z.block),
    ]
    mixed = pltpu.VMEM((z.tokens // lane_tile, z.block * z.local, lane_tile), f32)
    sums = pltpu.VMEM((z.local, z.block, z.block), f32)
    held = pltpu.VMEM((z.local, z.block, z.tokens), bf16)

    part = functools.partial

    first_pieces = gather_rows(right_one)
    outer_pieces = gather_rows(left_two)
    inner_pieces = gather_rows(left_one)
    second_pieces = gather_rows(right_two)
    count = len(first_pieces)

    upstream = exchange(run(part(turn_kernel, z), sends, [mixed], [ids, cotangent], 0))
    right_first, *parts = run(
        part(first_kernel, z, count), [weight] + sends, [mixed], [ids, tokens, *first_pieces], products
    )
    first_columns = exchange(parts)
    _, upstream_columns, *parts = run(
        part(middle_kernel, z, count, 1),
        [weight, acts] + sends,
        [mixed],
        [ids, *outer_pieces, *upstream],
        products,
    )
    second_rows = exchange(parts)
    left_first, columns, *parts = run(
        part(middle_kernel, z, count, 0),
        [weight, acts] + sends,
        [mixed],
        [ids, *inner_pieces, *first_columns],
        products,
    )
    preact = exchange(parts)
    right_second, hidden, second_back, *parts = run(
        part(gelu_kernel, z, count),
        [weight, acts, acts] + sends,
        [mixed],
        [ids, *second_pieces, *preact, *second_rows],
        products,
    )
    first_upstream = exchange(parts)
    parts = run(part(second_kernel, z), sends, [mixed], [ids, right_second, hidden], products)
    second_columns = exchange(parts)
    right_two_halves = run(part(grad_kernel, z), halves, [sums], [ids, hidden, second_back], products)
    _, upstream_rows, *parts = run(
        part(middle_kernel, z, 1, 1),
        [weight, acts] + sends,
        [mixed],
        [ids, left_first, *first_upstream],
        products,
    )
    first_rows = exchange(parts)
    left_two_halves = run(
        part(placed_grad_kernel, z), halves, [held, sums], [ids, upstream_columns, *second_columns], products
    )
    left_one_halves = run(part(grad_kernel, z), halves, [sums], [ids, columns, upstream_rows], products)
    turned, *right_one_halves = run(
        part(last_grad_kernel, z),
        [shaped(bf16, z.local, z.tokens, z.block)] + halves,
        [held, sums],
        [ids, tokens, *first_rows],
        products,
    )
    (tokens_grad,) = run(
        part(tokens_kernel, z),
        [shaped(bf16, z.tokens, z.local * z.block)],
        [],
        [right_first, turned],
        products,
    )
    summed = [
        scatter_rows(sent, kept, scale).reshape(z.local, z.rows, z.block)
        for sent, kept in (right_one_halves, left_one_halves, right_two_halves, left_two_halves)
    ]
    return (tokens_grad, *summed)


def solution(mesh):
    placed = (
        P("dp", "mp"),
        P("dp", "mp"),
        P("mp", "dp", None),
        P("mp", "dp", None),
        P("mp", "dp", None),
        P("mp", "dp", None),
    )
    return jax.shard_map(
        on_device,
        mesh=mesh,
        in_specs=placed,
        out_specs=(
            P("dp", "mp"),
            P("mp", "dp", None),
            P("mp", "dp", None),
            P("mp", "dp", None),
            P("mp", "dp", None),
        ),
        check_vma=False,
    )
```

```python
import functools
import math

import jax
import jax.numpy as jnp
from jax import lax
from jax.experimental import pallas as pl
from jax.experimental.pallas import tpu as pltpu
from jax.sharding import PartitionSpec as P

half_root = 0.7071067811865476
inv_root_tau = 0.3989422804014327
lane_tile = 128
packed_rows = 16
vmem_bytes = 14 * 1024 * 1024


def gelu_parts(values):
    normal_cdf = 0.5 * (1.0 + lax.erf(values * half_root))
    return (
        values * normal_cdf,
        normal_cdf + values * jnp.exp(-0.5 * values * values) * inv_root_tau,
    )


def hop(source, axis, offset):
    size = lax.axis_size(axis)
    return lax.ppermute(source, axis, [(i, i ^ offset) for i in range(size)])


def exchange(sends):
    return [sends[0]] + [hop(sends[q], "mp", q) for q in range(1, len(sends))]


def gather_rows(shards, after):
    size = lax.axis_size("dp")
    if shards.shape[2] % packed_rows:
        return [lax.all_gather(shards, "dp", axis=2, tiled=True)], after
    sent = [shards] * (size // 2)
    if after is not None:
        sent = [lax.optimization_barrier((shards, piece))[0] for piece in after]
    held = [shards] + [hop(sent[q], "dp", 2 * q) for q in range(1, size // 2)]
    other = [hop(piece, "dp", 1) for piece in held]
    return [piece for pair in zip(held, other) for piece in pair], held


def scatter_rows(sent, kept, scale):
    held = kept + hop(sent, "dp", 1).astype(jnp.float32)
    total = held[0]
    for q in range(1, held.shape[0]):
        total = total + hop(held[q].astype(jnp.bfloat16), "dp", 2 * q).astype(jnp.float32)
    return total * scale


class Sizes:
    def __init__(self, tokens, right_one):
        self.tokens = tokens.shape[0]
        self.local, self.rows, self.block = right_one.shape
        self.dp = lax.axis_size("dp")
        self.mp = lax.axis_size("mp")


def matmul(left, right, left_dim, right_dim):
    return lax.dot_general(
        left, right, (((left_dim,), (right_dim,)), ((), ())), preferred_element_type=jnp.float32
    )


def place(full, pieces, me):
    local, block, width = full.shape
    rows = block // len(pieces)
    for q, piece in enumerate(pieces):
        start = 0 if rows == block else pl.multiple_of((me ^ q) * rows, rows)
        full[:, pl.ds(start, rows), :] = piece[...].reshape(local, rows, width)


def spread(mixed, sends, index):
    size = sends[0].shape[0]
    for q, send in enumerate(sends):
        start = pl.multiple_of((index ^ q) * size, size)
        for h in range(mixed.shape[0]):
            lanes = slice(h * lane_tile, (h + 1) * lane_tile)
            send[:, lanes] = mixed[h, pl.ds(start, size), :].astype(jnp.bfloat16)


def split_grad(sums, sent, kept, index):
    pairs = sent.shape[0]
    local, block, width = sums.shape
    rows = block // (2 * pairs)
    for q in range(pairs):
        for target, offset in ((kept, 2 * q), (sent, 2 * q + 1)):
            start = pl.multiple_of((index ^ offset) * rows, rows)
            part = sums[:, pl.ds(start, rows), :].reshape(local * rows, width)
            target[q] = part.astype(target.dtype)


def column(mixed, c, local, value):
    for h in range(mixed.shape[0]):
        lanes = slice(h * lane_tile, (h + 1) * lane_tile)
        mixed[h, pl.ds(c, value.shape[0], stride=local), :] = value[:, lanes]


def turn_kernel(z, ids, cotangent, *refs):
    sends, (mixed,) = refs[: z.mp], refs[z.mp :]
    for c in range(z.local):
        part = cotangent[:, c * z.block : (c + 1) * z.block].astype(jnp.float32)
        column(mixed, c, z.local, part.T)
    spread(mixed, sends, ids[1])


def first_kernel(z, count, ids, tokens, *refs):
    pieces, refs = refs[:count], refs[count:]
    full, sends, mixed = refs[0], refs[1 : 1 + z.mp], refs[1 + z.mp]
    place(full, pieces, ids[0])
    for c in range(z.local):
        part = tokens[:, c * z.block : (c + 1) * z.block]
        column(mixed, c, z.local, matmul(full[c], part, 0, 1))
    spread(mixed, sends, ids[1])


def middle_kernel(z, count, side, ids, *refs):
    pieces, arrived, refs = refs[:count], refs[count : count + z.mp], refs[count + z.mp :]
    full, columns, sends, mixed = refs[0], refs[1], refs[2 : 2 + z.mp], refs[2 + z.mp]
    place(full, pieces, ids[0])
    place(columns, arrived, ids[1])
    for c in range(z.local):
        column(mixed, c, z.local, matmul(full[c], columns[c], side, 0))
    spread(mixed, sends, ids[1])


def gelu_kernel(z, count, ids, *refs):
    pieces, refs = refs[:count], refs[count:]
    preact, backs, refs = refs[: z.mp], refs[z.mp : 2 * z.mp], refs[2 * z.mp :]
    full, hidden, back, sends, mixed = refs[0], refs[1], refs[2], refs[3 : 3 + z.mp], refs[3 + z.mp]
    place(full, pieces, ids[0])
    place(hidden, preact, ids[1])
    place(back, backs, ids[1])
    for c in range(z.local):
        activated, slope = gelu_parts(hidden[c].astype(jnp.float32))
        hidden[c] = activated.astype(jnp.bfloat16)
        column(mixed, c, z.local, matmul(full[c], back[c], 1, 0) * slope)
    spread(mixed, sends, ids[1])


def second_kernel(z, ids, full, hidden, *refs):
    sends, (mixed,) = refs[: z.mp], refs[z.mp :]
    for c in range(z.local):
        column(mixed, c, z.local, matmul(full[c], hidden[c], 0, 0))
    spread(mixed, sends, ids[1])


def grad_kernel(z, ids, left, right, sent, kept, sums):
    for c in range(z.local):
        sums[c] = matmul(left[c], right[c], 1, 1)
    split_grad(sums, sent, kept, ids[0])


def placed_grad_kernel(z, ids, right, *refs):
    pieces, (sent, kept, left, sums) = refs[: z.mp], refs[z.mp :]
    place(left, pieces, ids[1])
    grad_kernel(z, ids, left, right, sent, kept, sums)


def last_grad_kernel(z, ids, tokens, *refs):
    pieces, (turned, sent, kept, back, sums) = refs[: z.mp], refs[z.mp :]
    place(back, pieces, ids[1])
    for c in range(z.local):
        block = back[c].T
        turned[c] = block
        sums[c] = matmul(tokens[:, c * z.block : (c + 1) * z.block], block, 0, 0)
    split_grad(sums, sent, kept, ids[0])


def tokens_kernel(z, full, turned, out):
    for c in range(z.local):
        part = matmul(turned[c], full[c], 1, 1)
        out[:, c * z.block : (c + 1) * z.block] = part.astype(jnp.bfloat16)


def shaped(kind, *shape):
    return jax.ShapeDtypeStruct(shape, kind)


def run(body, outs, scratch, inputs, products):
    specs = [
        pl.BlockSpec(memory_space=pltpu.SMEM if one.dtype == jnp.int32 else pltpu.VMEM) for one in inputs
    ]
    moved = sum(math.prod(one.shape) * one.dtype.itemsize for one in (*inputs, *outs))
    return pl.pallas_call(
        body,
        out_shape=outs,
        in_specs=specs,
        out_specs=[pl.BlockSpec(memory_space=pltpu.VMEM) for _ in outs],
        scratch_shapes=scratch,
        compiler_params=pltpu.CompilerParams(vmem_limit_bytes=vmem_bytes),
        cost_estimate=pl.CostEstimate(flops=2 * products, bytes_accessed=moved, transcendentals=0),
    )(*inputs)


def on_device(tokens, cotangent, right_one, left_one, right_two, left_two):
    z = Sizes(tokens, right_one)
    bf16, f32 = jnp.bfloat16, jnp.float32
    scale = 1.0 / math.sqrt(z.tokens * z.dp)
    ids = jnp.stack([lax.axis_index("dp"), lax.axis_index("mp")]).astype(jnp.int32)
    products = z.local * z.block * z.block * z.tokens
    weight = shaped(bf16, z.local, z.block, z.block)
    acts = shaped(bf16, z.local, z.block, z.tokens)
    sends = [shaped(bf16, z.local * z.local, z.tokens)] * z.mp
    halves = [
        shaped(bf16, z.dp // 2, z.local * z.rows, z.block),
        shaped(f32, z.dp // 2, z.local * z.rows, z.block),
    ]
    mixed = pltpu.VMEM((z.tokens // lane_tile, z.block * z.local, lane_tile), f32)
    sums = pltpu.VMEM((z.local, z.block, z.block), f32)
    held = pltpu.VMEM((z.local, z.block, z.tokens), bf16)

    part = functools.partial

    def part_of(pieces, which):
        return [piece[which] for piece in pieces]

    first, after = gather_rows(right_one[None], None)
    outer, after = gather_rows(left_two[None], after)
    inner, after = gather_rows(left_one[None], after)
    second, after = gather_rows(right_two[None], after)
    first_pieces, outer_pieces = part_of(first, 0), part_of(outer, 0)
    inner_pieces, second_pieces = part_of(inner, 0), part_of(second, 0)

    upstream = exchange(run(part(turn_kernel, z), sends, [mixed], [ids, cotangent], 0))
    right_first, *parts = run(
        part(first_kernel, z, len(first_pieces)),
        [weight] + sends,
        [mixed],
        [ids, tokens, *first_pieces], products
    )
    first_columns = exchange(parts)
    _, upstream_columns, *parts = run(
        part(middle_kernel, z, len(outer_pieces), 1),
        [weight, acts] + sends,
        [mixed],
        [ids, *outer_pieces, *upstream],
        products,
    )
    second_rows = exchange(parts)
    left_first, columns, *parts = run(
        part(middle_kernel, z, len(inner_pieces), 0),
        [weight, acts] + sends,
        [mixed],
        [ids, *inner_pieces, *first_columns],
        products,
    )
    preact = exchange(parts)
    right_second, hidden, second_back, *parts = run(
        part(gelu_kernel, z, len(second_pieces)),
        [weight, acts, acts] + sends,
        [mixed],
        [ids, *second_pieces, *preact, *second_rows],
        products,
    )
    first_upstream = exchange(parts)
    parts = run(part(second_kernel, z), sends, [mixed], [ids, right_second, hidden], products)
    second_columns = exchange(parts)
    right_two_halves = run(part(grad_kernel, z), halves, [sums], [ids, hidden, second_back], products)
    _, upstream_rows, *parts = run(
        part(middle_kernel, z, 1, 1),
        [weight, acts] + sends,
        [mixed],
        [ids, left_first, *first_upstream],
        products,
    )
    first_rows = exchange(parts)
    left_two_halves = run(
        part(placed_grad_kernel, z), halves, [held, sums], [ids, upstream_columns, *second_columns], products
    )
    left_one_halves = run(part(grad_kernel, z), halves, [sums], [ids, columns, upstream_rows], products)
    turned, *right_one_halves = run(
        part(last_grad_kernel, z),
        [shaped(bf16, z.local, z.tokens, z.block)] + halves,
        [held, sums],
        [ids, tokens, *first_rows],
        products,
    )
    (tokens_grad,) = run(
        part(tokens_kernel, z),
        [shaped(bf16, z.tokens, z.local * z.block)],
        [],
        [right_first, turned],
        products,
    )
    summed = [
        scatter_rows(sent, kept, scale).reshape(z.local, z.rows, z.block)
        for sent, kept in (right_one_halves, left_one_halves, right_two_halves, left_two_halves)
    ]
    return (tokens_grad, *summed)


def solution(mesh):
    placed = (
        P("dp", "mp"),
        P("dp", "mp"),
        P("mp", "dp", None),
        P("mp", "dp", None),
        P("mp", "dp", None),
        P("mp", "dp", None),
    )
    return jax.shard_map(
        on_device,
        mesh=mesh,
        in_specs=placed,
        out_specs=(
            P("dp", "mp"),
            P("mp", "dp", None),
            P("mp", "dp", None),
            P("mp", "dp", None),
            P("mp", "dp", None),
        ),
        check_vma=False,
    )
```

```python
import functools
import math

import jax
import jax.numpy as jnp
from jax import lax
from jax.experimental import pallas as pl
from jax.experimental.pallas import tpu as pltpu
from jax.sharding import PartitionSpec as P

half_root = 0.7071067811865476
inv_root_tau = 0.3989422804014327
lane_tile = 128
packed_rows = 16
CFG = {'flops': 2, 'near': (True, True, False), 'scatters': {'first': 'direct', 'inner': 'direct', 'outer': 'direct', 'second': 'direct'}, 'A1': 0, 'A2': 0, 'A3': 0, 'A4': 0, 'A5': 0, 'A6': 0, 'A7': 1, 'B1': 0, 'B2': 0, 'B3': 0, 'B4': 0, 'B5': 0, 'B6': 0, 'B7': 0, 'C1': 0, 'C2': 0, 'C3': 0, 'C4': 0, 'T1': 0, 'T2': 0, 'T3': 0, 'T4': 0, 'T5': 0, 'T6': 0, 'Q1': 0, 'Q2': 0, 'Q3': 0, 'Q4': 0, 'Q5': 0, 'Q6': 0}
vmem_bytes = 14 * 1024 * 1024


def gelu_parts(values):
    normal_cdf = 0.5 * (1.0 + lax.erf(values * half_root))
    return (
        values * normal_cdf,
        normal_cdf + values * jnp.exp(-0.5 * values * values) * inv_root_tau,
    )


def hop(source, axis, offset):
    size = lax.axis_size(axis)
    return lax.ppermute(source, axis, [(i, i ^ offset) for i in range(size)])


def exchange(sends):
    return [sends[0]] + [hop(sends[q], "mp", q) for q in range(1, len(sends))]


def nothing_kernel(*refs):
    pass


def wait_for(source, *others):
    if not others:
        return source
    return pl.pallas_call(
        nothing_kernel,
        out_shape=shaped(source.dtype, *source.shape),
        in_specs=[pl.BlockSpec(memory_space=pl.ANY)] * (1 + len(others)),
        out_specs=pl.BlockSpec(memory_space=pl.ANY),
        input_output_aliases={0: 0},
        compiler_params=pltpu.CompilerParams(vmem_limit_bytes=vmem_bytes),
    )(source, *others)


def steps_of(size):
    return [1 << bit for bit in reversed(range(1, size.bit_length() - 1))]


class Pieces:
    def __init__(self, shard):
        self.size = lax.axis_size("dp")
        self.depth = 0
        self.whole = None
        self.got = {0: shard[None]}
        if shard.shape[1] % packed_rows:
            self.whole = lax.all_gather(shard, "dp", axis=1, tiled=True)[None]

    def wave(self, *others):
        self.depth += 1
        offsets = [o for o in range(self.size) if o.bit_count() == self.depth]
        if self.whole is not None:
            return []
        for o in offsets:
            low = o & -o
            self.got[o] = hop(wait_for(self.got[o ^ low], *others), "dp", low)
        return [self.got[o] for o in offsets]

    def finish(self):
        if self.whole is not None:
            return ((0,),), (self.whole,)
        while len(self.got) < self.size:
            self.wave()
        return tuple((o,) for o in self.got), tuple(self.got.values())


class Joined:
    def __init__(self, shard, near):
        self.steps = steps_of(lax.axis_size("dp"))
        self.steps.insert(0 if near else len(self.steps), 1)
        self.offsets, self.held = (0,), shard[None]
        self.arrived = None
        if shard.shape[1] % packed_rows:
            self.steps = []
            self.held = lax.all_gather(shard, "dp", axis=1, tiled=True)[None]

    def step(self, *others):
        if not self.steps:
            return []
        if self.arrived is not None:
            self.held = join(self.held, self.arrived, others)
            self.offsets += self.new
            others = ()
        step = self.steps.pop(0)
        self.new = tuple(o ^ step for o in self.offsets)
        self.arrived = hop(wait_for(self.held, *others), "dp", step)
        return [self.arrived]

    def finish(self):
        while self.steps:
            self.step()
        if self.arrived is None:
            return ((0,),), (self.held,)
        return (self.offsets, self.new), (self.held, self.arrived)


class Scatter:
    def __init__(self, halves, steps, direct):
        self.sent, self.kept = halves
        self.steps = list(steps)
        self.direct = direct
        self.held = None

    def step(self, *others):
        step = self.steps.pop(0)
        if self.held is not None:
            half = self.held.shape[0] // 2
            self.sent, self.kept = self.held[half:].astype(jnp.bfloat16), self.held[:half]
        self.held = self.kept + hop(wait_for(self.sent, *others), "dp", step).astype(jnp.float32)
        return self.held

    def finish(self, *others):
        if not self.direct:
            while self.steps:
                self.step(*others)
            return self.held[0]
        size = self.held.shape[0]
        bits = list(reversed(self.steps))
        offsets = [sum(bit for k, bit in enumerate(bits) if q >> k & 1) for q in range(size)]
        total = self.held[0]
        for q in range(1, size):
            part = wait_for(self.held[q].astype(jnp.bfloat16), *others)
            total = total + hop(part, "dp", offsets[q]).astype(jnp.float32)
        return total


def join_kernel(one, two, out):
    out[: one.shape[0]] = one[...]
    out[one.shape[0] :] = two[...]


def join(one, two, after):
    count = one.shape[0] + two.shape[0]
    (out,) = run(join_kernel, [shaped(one.dtype, count, *one.shape[1:])], [], [one, two], 0, after)
    return out


class Sizes:
    def __init__(self, tokens, right_one):
        self.tokens = tokens.shape[0]
        self.local, self.rows, self.block = right_one.shape
        self.dp = lax.axis_size("dp")
        self.mp = lax.axis_size("mp")


def matmul(left, right, left_dim, right_dim):
    return lax.dot_general(
        left, right, (((left_dim,), (right_dim,)), ((), ())), preferred_element_type=jnp.float32
    )


def place(full, pieces, layout, me):
    local, block, width = full.shape
    rows = block // sum(len(offsets) for offsets in layout)
    for piece, offsets in zip(pieces, layout, strict=True):
        for k, offset in enumerate(offsets):
            start = 0 if rows == block else pl.multiple_of((me ^ offset) * rows, rows)
            full[:, pl.ds(start, rows), :] = piece[k].reshape(local, rows, width)


def place_arrived(full, pieces, me):
    local, block, width = full.shape
    rows = block // len(pieces)
    for q, piece in enumerate(pieces):
        start = pl.multiple_of((me ^ q) * rows, rows)
        full[:, pl.ds(start, rows), :] = piece[...].reshape(local, rows, width)


def spread(mixed, sends, index):
    size = sends[0].shape[0]
    for q, send in enumerate(sends):
        start = pl.multiple_of((index ^ q) * size, size)
        for h in range(mixed.shape[0]):
            lanes = slice(h * lane_tile, (h + 1) * lane_tile)
            send[:, lanes] = mixed[h, pl.ds(start, size), :].astype(jnp.bfloat16)


def split_grad(sums, sent, kept, index, steps):
    local, block, width = sums.shape
    offsets = [0]
    for step in reversed(steps[1:]):
        offsets += [offset ^ step for offset in offsets]
    rows = block // (2 * len(offsets))
    for q, offset in enumerate(offsets):
        for target, number in ((kept, offset), (sent, offset ^ steps[0])):
            start = pl.multiple_of((index ^ number) * rows, rows)
            part = sums[:, pl.ds(start, rows), :].reshape(local * rows, width)
            target[q] = part.astype(target.dtype)


def column(mixed, c, local, value):
    for h in range(mixed.shape[0]):
        lanes = slice(h * lane_tile, (h + 1) * lane_tile)
        mixed[h, pl.ds(c, value.shape[0], stride=local), :] = value[:, lanes]


def turn_kernel(z, ids, cotangent, *refs):
    sends, (mixed,) = refs[: z.mp], refs[z.mp :]
    for c in range(z.local):
        part = cotangent[:, c * z.block : (c + 1) * z.block].astype(jnp.float32)
        column(mixed, c, z.local, part.T)
    spread(mixed, sends, ids[1])


def first_kernel(z, layout, ids, tokens, *refs):
    pieces, refs = refs[: len(layout)], refs[len(layout) :]
    full, sends, mixed = refs[0], refs[1 : 1 + z.mp], refs[1 + z.mp]
    place(full, pieces, layout, ids[0])
    for c in range(z.local):
        part = tokens[:, c * z.block : (c + 1) * z.block]
        column(mixed, c, z.local, matmul(full[c], part, 0, 1))
    spread(mixed, sends, ids[1])


def middle_kernel(z, layout, side, ids, *refs):
    pieces, refs = refs[: len(layout)], refs[len(layout) :]
    arrived, refs = refs[: z.mp], refs[z.mp :]
    full, columns, sends, mixed = refs[0], refs[1], refs[2 : 2 + z.mp], refs[2 + z.mp]
    place(full, pieces, layout, ids[0])
    place_arrived(columns, arrived, ids[1])
    for c in range(z.local):
        column(mixed, c, z.local, matmul(full[c], columns[c], side, 0))
    spread(mixed, sends, ids[1])


def gelu_kernel(z, layout, ids, *refs):
    pieces, refs = refs[: len(layout)], refs[len(layout) :]
    preact, backs, refs = refs[: z.mp], refs[z.mp : 2 * z.mp], refs[2 * z.mp :]
    full, hidden, back, sends, mixed = refs[0], refs[1], refs[2], refs[3 : 3 + z.mp], refs[3 + z.mp]
    place(full, pieces, layout, ids[0])
    place_arrived(hidden, preact, ids[1])
    place_arrived(back, backs, ids[1])
    for c in range(z.local):
        activated, slope = gelu_parts(hidden[c].astype(jnp.float32))
        hidden[c] = activated.astype(jnp.bfloat16)
        column(mixed, c, z.local, matmul(full[c], back[c], 1, 0) * slope)
    spread(mixed, sends, ids[1])


def second_kernel(z, ids, full, hidden, *refs):
    sends, (mixed,) = refs[: z.mp], refs[z.mp :]
    for c in range(z.local):
        column(mixed, c, z.local, matmul(full[c], hidden[c], 0, 0))
    spread(mixed, sends, ids[1])


def grad_kernel(z, steps, ids, left, right, sent, kept, sums):
    for c in range(z.local):
        sums[c] = matmul(left[c], right[c], 1, 1)
    split_grad(sums, sent, kept, ids[0], steps)


def placed_grad_kernel(z, steps, ids, right, *refs):
    pieces, (sent, kept, left, sums) = refs[: z.mp], refs[z.mp :]
    place_arrived(left, pieces, ids[1])
    grad_kernel(z, steps, ids, left, right, sent, kept, sums)


def last_grad_kernel(z, steps, ids, tokens, *refs):
    pieces, (turned, sent, kept, back, sums) = refs[: z.mp], refs[z.mp :]
    place_arrived(back, pieces, ids[1])
    for c in range(z.local):
        block = back[c].T
        turned[c] = block
        sums[c] = matmul(tokens[:, c * z.block : (c + 1) * z.block], block, 0, 0)
    split_grad(sums, sent, kept, ids[0], steps)


def tokens_kernel(z, full, turned, out):
    for c in range(z.local):
        part = matmul(turned[c], full[c], 1, 1)
        out[:, c * z.block : (c + 1) * z.block] = part.astype(jnp.bfloat16)


def shaped(kind, *shape):
    return jax.ShapeDtypeStruct(shape, kind)


def run(body, outs, scratch, inputs, products, after=()):
    def skip(*refs):
        body(*refs[: len(inputs)], *refs[len(inputs) + len(after) :])

    specs = [
        pl.BlockSpec(memory_space=pltpu.SMEM if one.dtype == jnp.int32 else pltpu.VMEM) for one in inputs
    ]
    moved = sum(math.prod(one.shape) * one.dtype.itemsize for one in (*inputs, *outs))
    return pl.pallas_call(
        skip,
        out_shape=outs,
        in_specs=specs + [pl.BlockSpec(memory_space=pl.ANY)] * len(after),
        out_specs=[pl.BlockSpec(memory_space=pltpu.VMEM) for _ in outs],
        scratch_shapes=scratch,
        compiler_params=pltpu.CompilerParams(vmem_limit_bytes=vmem_bytes),
        cost_estimate=pl.CostEstimate(flops=CFG["flops"] * products, bytes_accessed=moved, transcendentals=0),
    )(*inputs, *after)


def on_device(tokens, cotangent, right_one, left_one, right_two, left_two):
    z = Sizes(tokens, right_one)
    bf16, f32 = jnp.bfloat16, jnp.float32
    scale = 1.0 / math.sqrt(z.tokens * z.dp)
    ids = jnp.stack([lax.axis_index("dp"), lax.axis_index("mp")]).astype(jnp.int32)
    products = z.local * z.block * z.block * z.tokens
    weight = shaped(bf16, z.local, z.block, z.block)
    acts = shaped(bf16, z.local, z.block, z.tokens)
    sends = [shaped(bf16, z.local * z.local, z.tokens)] * z.mp
    halves = [
        shaped(bf16, z.dp // 2, z.local * z.rows, z.block),
        shaped(f32, z.dp // 2, z.local * z.rows, z.block),
    ]
    mixed = pltpu.VMEM((z.tokens // lane_tile, z.block * z.local, lane_tile), f32)
    sums = pltpu.VMEM((z.local, z.block, z.block), f32)
    held = pltpu.VMEM((z.local, z.block, z.tokens), bf16)

    part = functools.partial
    along = list(reversed(steps_of(z.dp)))
    orders = {name: [*along, 1] if kind == "far" else [1, *along] for name, kind in CFG["scatters"].items()}

    def on(key, *values):
        return values if CFG[key] else ()

    near = CFG["near"]
    first, inner = Pieces(right_one), Joined(left_one, near[0])
    outer, second = Joined(left_two, near[1]), Joined(right_two, near[2])

    wave0 = first.wave()
    i0 = inner.step()
    turned_up = run(part(turn_kernel, z), sends, [mixed], [ids, cotangent], 0)
    upstream = exchange(turned_up)
    wave1 = first.wave()
    o0 = outer.step() if near[1] else outer.step(*on("A1", *wave0[:1]))
    i1 = inner.step(*on("A2", turned_up[1]))
    s0 = second.step(*on("A3", *wave0[:1])) if not near[2] else second.step()
    wave2 = first.wave()
    first_layout, first_pieces = first.finish()
    right_first, *parts = run(
        part(first_kernel, z, first_layout),
        [weight] + sends,
        [mixed],
        [ids, tokens, *first_pieces],
        products,
        [*on("A4", *s0), *on("A5", *i1), *on("A6", *o0), *on("A7", *upstream[2:3])],
    )
    k1 = parts[1]
    first_columns = exchange(parts)
    i2 = inner.step(*on("B1", *wave2))
    o1 = outer.step(*on("B2", k1), *on("B3", first_columns[1]))
    s1 = second.step(*on("B4", k1), *on("B5", first_columns[1]))
    inner_layout, inner_pieces = inner.finish()
    left_first, columns, *parts = run(
        part(middle_kernel, z, inner_layout, 0),
        [weight, acts] + sends,
        [mixed],
        [ids, *inner_pieces, *first_columns],
        products,
        [*on("B6", *s1), *on("B7", *o1)],
    )
    k3 = parts[1]
    preact = exchange(parts)
    outer.step(*on("C1", k3))
    second.step(*on("C2", k3))
    outer_layout, outer_pieces = outer.finish()
    second_layout, second_pieces = second.finish()
    _, upstream_columns, *parts = run(
        part(middle_kernel, z, outer_layout, 1),
        [weight, acts] + sends,
        [mixed],
        [ids, *outer_pieces, *upstream],
        products,
        [*on("C3", k3), *on("C4", preact[1])],
    )
    second_rows = exchange(parts)
    right_second, hidden, second_back, *parts = run(
        part(gelu_kernel, z, second_layout),
        [weight, acts, acts] + sends,
        [mixed],
        [ids, *second_pieces, *preact, *second_rows],
        products,
    )
    first_upstream = exchange(parts)
    parts = run(
        part(second_kernel, z),
        sends,
        [mixed],
        [ids, right_second, hidden],
        products,
        [*on("T1", first_upstream[1])],
    )
    second_columns = exchange(parts)
    right_two_halves = run(
        part(grad_kernel, z, orders["second"]),
        halves,
        [sums],
        [ids, hidden, second_back],
        products,
        [*on("T2", first_upstream[1]), *on("T3", second_columns[1])],
    )
    scatter = {"second": Scatter(right_two_halves, orders["second"], CFG["scatters"]["second"] == "direct")}
    scatter["second"].step()
    _, upstream_rows, *parts = run(
        part(middle_kernel, z, ((0,),), 1),
        [weight, acts] + sends,
        [mixed],
        [ids, left_first[None], *first_upstream],
        products,
        [*on("T4", *right_two_halves[:1])],
    )
    left_one_halves = run(part(grad_kernel, z, orders["inner"]), halves, [sums], [ids, columns, upstream_rows], products)
    parts[1] = wait_for(parts[1], *on("T5", left_one_halves[0]))
    first_rows = exchange(parts)
    scatter["inner"] = Scatter(left_one_halves, orders["inner"], CFG["scatters"]["inner"] == "direct")
    scatter["inner"].step()
    left_two_halves = run(
        part(placed_grad_kernel, z, orders["outer"]),
        halves,
        [held, sums],
        [ids, upstream_columns, *second_columns],
        products,
        [*on("T6", first_rows[1])],
    )
    scatter["outer"] = Scatter(left_two_halves, orders["outer"], CFG["scatters"]["outer"] == "direct")
    o_held = scatter["outer"].step()
    totals = {"second": scatter["second"].finish()}
    turned, *right_one_halves = run(
        part(last_grad_kernel, z, orders["first"]),
        [shaped(bf16, z.local, z.tokens, z.block)] + halves,
        [held, sums],
        [ids, tokens, *first_rows],
        products,
        [*on("Q1", totals["second"]), *on("Q2", left_two_halves[0]), *on("Q3", scatter["inner"].held)],
    )
    scatter["first"] = Scatter(right_one_halves, orders["first"], CFG["scatters"]["first"] == "direct")
    f_held = scatter["first"].step()
    totals["inner"] = scatter["inner"].finish()
    totals["first"] = scatter["first"].finish(*on("Q4", totals["inner"]), *on("Q5", o_held))
    totals["outer"] = scatter["outer"].finish()
    (tokens_grad,) = run(
        part(tokens_kernel, z),
        [shaped(bf16, z.tokens, z.local * z.block)],
        [],
        [right_first, turned],
        products,
        [*on("Q6", f_held)],
    )
    summed = [
        (totals[name] * scale).reshape(z.local, z.rows, z.block) for name in ("first", "inner", "second", "outer")
    ]
    return (tokens_grad, *summed)


def solution(mesh):
    placed = (
        P("dp", "mp"),
        P("dp", "mp"),
        P("mp", "dp", None),
        P("mp", "dp", None),
        P("mp", "dp", None),
        P("mp", "dp", None),
    )
    return jax.shard_map(
        on_device,
        mesh=mesh,
        in_specs=placed,
        out_specs=(
            P("dp", "mp"),
            P("mp", "dp", None),
            P("mp", "dp", None),
            P("mp", "dp", None),
            P("mp", "dp", None),
        ),
        check_vma=False,
    )
```

```python
import functools
import math

import jax
import jax.numpy as jnp
from jax import lax
from jax.experimental import pallas as pl
from jax.experimental.pallas import tpu as pltpu
from jax.sharding import PartitionSpec as P

half_root = 0.7071067811865476
inv_root_tau = 0.3989422804014327
lane_tile = 128
packed_rows = 16
CFG = {'flops': 2, 'near': (True, True, False), 'scatters': {'first': 'direct', 'inner': 'direct', 'outer': 'direct', 'second': 'direct'}, 'A1': 0, 'A2': 0, 'A3': 0, 'A4': 0, 'A5': 0, 'A6': 0, 'A7': 1, 'B1': 0, 'B2': 0, 'B3': 0, 'B4': 0, 'B5': 0, 'B6': 0, 'B7': 0, 'C1': 0, 'C2': 0, 'C3': 0, 'C4': 0, 'T1': 0, 'T2': 0, 'T3': 0, 'T4': 0, 'T5': 1, 'T6': 0, 'Q1': 0, 'Q2': 0, 'Q3': 1, 'Q4': 0, 'Q5': 0, 'Q6': 0, 'Q7': 0, 'Q8': 0, 'Q9': 0, 'A8': 0, 'A9': 0, 'B8': 0, 'B9': 0, 'D1': 0, 'D2': 0, 'E1': 0, 'E2': 0, 'E3': 0, 'E4': 0, 'T8': 0, 'T9': 0, 'T10': 0, 'T11': 0, 'T12': 0, 'T13': 0, 'T14': 0, 'T15': 0, 'T16': 0, 'BA': 0, 'BC': 0, 'S': 0, 'S1': 0, 'S2': 0, 'S3': 0, 'S4': 0, 'S5': 0, 'pair': 0}
vmem_bytes = 14 * 1024 * 1024


def gelu_parts(values):
    normal_cdf = 0.5 * (1.0 + lax.erf(values * half_root))
    return (
        values * normal_cdf,
        normal_cdf + values * jnp.exp(-0.5 * values * values) * inv_root_tau,
    )


def hop(source, axis, offset):
    size = lax.axis_size(axis)
    return lax.ppermute(source, axis, [(i, i ^ offset) for i in range(size)])


def exchange(sends):
    return [sends[0]] + [hop(sends[q], "mp", q) for q in range(1, len(sends))]


def nothing_kernel(*refs):
    pass


def wait_for(source, *others):
    if not others:
        return source
    return pl.pallas_call(
        nothing_kernel,
        out_shape=shaped(source.dtype, *source.shape),
        in_specs=[pl.BlockSpec(memory_space=pl.ANY)] * (1 + len(others)),
        out_specs=pl.BlockSpec(memory_space=pl.ANY),
        input_output_aliases={0: 0},
        compiler_params=pltpu.CompilerParams(vmem_limit_bytes=vmem_bytes),
    )(source, *others)


def steps_of(size):
    return [1 << bit for bit in reversed(range(1, size.bit_length() - 1))]


class Pieces:
    def __init__(self, shard):
        self.size = lax.axis_size("dp")
        self.depth = 0
        self.whole = None
        self.got = {0: shard[None]}
        if shard.shape[1] % packed_rows:
            self.whole = lax.all_gather(shard, "dp", axis=1, tiled=True)[None]

    def wave(self, *others):
        self.depth += 1
        offsets = [o for o in range(self.size) if o.bit_count() == self.depth]
        if self.whole is not None:
            return []
        for o in offsets:
            low = o & -o
            self.got[o] = hop(wait_for(self.got[o ^ low], *others), "dp", low)
        return [self.got[o] for o in offsets]

    def finish(self):
        if self.whole is not None:
            return ((0,),), (self.whole,)
        while len(self.got) < self.size:
            self.wave()
        return tuple((o,) for o in self.got), tuple(self.got.values())


class Joined:
    def __init__(self, shard, near):
        self.steps = steps_of(lax.axis_size("dp"))
        self.steps.insert(0 if near else len(self.steps), 1)
        self.offsets, self.held = (0,), shard[None]
        self.arrived = None
        if shard.shape[-2] % packed_rows:
            self.steps = []
            self.held = lax.all_gather(shard, "dp", axis=shard.ndim - 2, tiled=True)[None]

    def step(self, *others):
        if not self.steps:
            return []
        if self.arrived is not None:
            self.held = join(self.held, self.arrived, others)
            self.offsets += self.new
            others = ()
        step = self.steps.pop(0)
        self.new = tuple(o ^ step for o in self.offsets)
        self.arrived = hop(wait_for(self.held, *others), "dp", step)
        return [self.arrived]

    def finish(self):
        while self.steps:
            self.step()
        if self.arrived is None:
            return ((0,),), (self.held,)
        return (self.offsets, self.new), (self.held, self.arrived)


class Scatter:
    def __init__(self, halves, steps, direct):
        self.sent, self.kept = halves
        self.steps = list(steps)
        self.direct = direct
        self.held = None

    def step(self, *others):
        step = self.steps.pop(0)
        if self.held is not None:
            half = self.held.shape[0] // 2
            self.sent, self.kept = self.held[half:].astype(jnp.bfloat16), self.held[:half]
        self.held = self.kept + hop(wait_for(self.sent, *others), "dp", step).astype(jnp.float32)
        return self.held

    def send(self, *others):
        size = self.held.shape[0]
        bits = list(reversed(self.steps))
        self.total = self.held[0]
        self.pieces = []
        for q in range(1, size):
            part = wait_for(self.held[q].astype(jnp.bfloat16), *others)
            self.pieces.append(hop(part, "dp", sum(bit for k, bit in enumerate(bits) if q >> k & 1)))
        return self.pieces

    def collect(self, scale, *others):
        body = functools.partial(total_kernel, scale)
        (out,) = run(body, [shaped(jnp.float32, *self.total.shape)], [], [self.total, *self.pieces], 0, others)
        return out

    def finish(self, *others):
        if not self.direct:
            while self.steps:
                self.step(*others)
            return self.held[0]
        size = self.held.shape[0]
        bits = list(reversed(self.steps))
        offsets = [sum(bit for k, bit in enumerate(bits) if q >> k & 1) for q in range(size)]
        total = self.held[0]
        for q in range(1, size):
            part = wait_for(self.held[q].astype(jnp.bfloat16), *others)
            total = total + hop(part, "dp", offsets[q]).astype(jnp.float32)
        return total


def join_kernel(one, two, out):
    out[: one.shape[0]] = one[...]
    out[one.shape[0] :] = two[...]


def join(one, two, after):
    count = one.shape[0] + two.shape[0]
    (out,) = run(join_kernel, [shaped(one.dtype, count, *one.shape[1:])], [], [one, two], 0, after)
    return out


class Sizes:
    def __init__(self, tokens, right_one):
        self.tokens = tokens.shape[0]
        self.local, self.rows, self.block = right_one.shape
        self.dp = lax.axis_size("dp")
        self.mp = lax.axis_size("mp")


def matmul(left, right, left_dim, right_dim):
    return lax.dot_general(
        left, right, (((left_dim,), (right_dim,)), ((), ())), preferred_element_type=jnp.float32
    )


def place(full, pieces, layout, me, which):
    local, block, width = full.shape
    rows = block // sum(len(offsets) for offsets in layout)
    for piece, offsets in zip(pieces, layout, strict=True):
        for k, offset in enumerate(offsets):
            start = 0 if rows == block else pl.multiple_of((me ^ offset) * rows, rows)
            part = piece[k] if which is None else piece[k, which]
            full[:, pl.ds(start, rows), :] = part.reshape(local, rows, width)


def place_arrived(full, pieces, me):
    local, block, width = full.shape
    rows = block // len(pieces)
    for q, piece in enumerate(pieces):
        start = pl.multiple_of((me ^ q) * rows, rows)
        full[:, pl.ds(start, rows), :] = piece[...].reshape(local, rows, width)


def spread(mixed, sends, index):
    size = sends[0].shape[0]
    for q, send in enumerate(sends):
        start = pl.multiple_of((index ^ q) * size, size)
        for h in range(mixed.shape[0]):
            lanes = slice(h * lane_tile, (h + 1) * lane_tile)
            send[:, lanes] = mixed[h, pl.ds(start, size), :].astype(jnp.bfloat16)


def split_grad(sums, sent, kept, index, steps):
    local, block, width = sums.shape
    offsets = [0]
    for step in reversed(steps[1:]):
        offsets += [offset ^ step for offset in offsets]
    rows = block // (2 * len(offsets))
    for q, offset in enumerate(offsets):
        for target, number in ((kept, offset), (sent, offset ^ steps[0])):
            start = pl.multiple_of((index ^ number) * rows, rows)
            part = sums[:, pl.ds(start, rows), :].reshape(local * rows, width)
            target[q] = part.astype(target.dtype)


def column(mixed, c, local, value):
    for h in range(mixed.shape[0]):
        lanes = slice(h * lane_tile, (h + 1) * lane_tile)
        mixed[h, pl.ds(c, value.shape[0], stride=local), :] = value[:, lanes]


def turn_kernel(z, ids, cotangent, *refs):
    sends, (mixed,) = refs[: z.mp], refs[z.mp :]
    for c in range(z.local):
        part = cotangent[:, c * z.block : (c + 1) * z.block].astype(jnp.float32)
        column(mixed, c, z.local, part.T)
    spread(mixed, sends, ids[1])


def first_kernel(z, layout, which, ids, tokens, *refs):
    pieces, refs = refs[: len(layout)], refs[len(layout) :]
    full, sends, mixed = refs[0], refs[1 : 1 + z.mp], refs[1 + z.mp]
    place(full, pieces, layout, ids[0], which)
    for c in range(z.local):
        part = tokens[:, c * z.block : (c + 1) * z.block]
        column(mixed, c, z.local, matmul(full[c], part, 0, 1))
    spread(mixed, sends, ids[1])


def middle_kernel(z, layout, which, side, ids, *refs):
    pieces, refs = refs[: len(layout)], refs[len(layout) :]
    arrived, refs = refs[: z.mp], refs[z.mp :]
    full, columns, sends, mixed = refs[0], refs[1], refs[2 : 2 + z.mp], refs[2 + z.mp]
    place(full, pieces, layout, ids[0], which)
    place_arrived(columns, arrived, ids[1])
    for c in range(z.local):
        column(mixed, c, z.local, matmul(full[c], columns[c], side, 0))
    spread(mixed, sends, ids[1])


def back_kernel(z, ids, full, *refs):
    arrived, refs = refs[: z.mp], refs[z.mp :]
    columns, sends, mixed = refs[0], refs[1 : 1 + z.mp], refs[1 + z.mp]
    place_arrived(columns, arrived, ids[1])
    for c in range(z.local):
        column(mixed, c, z.local, matmul(full[c], columns[c], 1, 0))
    spread(mixed, sends, ids[1])


def gelu_kernel(z, layout, which, ids, *refs):
    pieces, refs = refs[: len(layout)], refs[len(layout) :]
    preact, backs, refs = refs[: z.mp], refs[z.mp : 2 * z.mp], refs[2 * z.mp :]
    full, hidden, back, sends, mixed = refs[0], refs[1], refs[2], refs[3 : 3 + z.mp], refs[3 + z.mp]
    place(full, pieces, layout, ids[0], which)
    place_arrived(hidden, preact, ids[1])
    place_arrived(back, backs, ids[1])
    for c in range(z.local):
        activated, slope = gelu_parts(hidden[c].astype(jnp.float32))
        hidden[c] = activated.astype(jnp.bfloat16)
        column(mixed, c, z.local, matmul(full[c], back[c], 1, 0) * slope)
    spread(mixed, sends, ids[1])


def second_kernel(z, ids, full, hidden, *refs):
    sends, (mixed,) = refs[: z.mp], refs[z.mp :]
    for c in range(z.local):
        column(mixed, c, z.local, matmul(full[c], hidden[c], 0, 0))
    spread(mixed, sends, ids[1])


def grad_kernel(z, steps, ids, left, right, sent, kept, sums):
    for c in range(z.local):
        sums[c] = matmul(left[c], right[c], 1, 1)
    split_grad(sums, sent, kept, ids[0], steps)


def placed_grad_kernel(z, steps, ids, right, *refs):
    pieces, (sent, kept, left, sums) = refs[: z.mp], refs[z.mp :]
    place_arrived(left, pieces, ids[1])
    grad_kernel(z, steps, ids, left, right, sent, kept, sums)


def last_grad_kernel(z, steps, ids, tokens, *refs):
    pieces, (turned, sent, kept, back, sums) = refs[: z.mp], refs[z.mp :]
    place_arrived(back, pieces, ids[1])
    for c in range(z.local):
        block = back[c].T
        turned[c] = block
        sums[c] = matmul(tokens[:, c * z.block : (c + 1) * z.block], block, 0, 0)
    split_grad(sums, sent, kept, ids[0], steps)


def total_kernel(scale, held, *refs):
    pieces, out = refs[:-1], refs[-1]
    total = held[...]
    for piece in pieces:
        total += piece[...].astype(jnp.float32)
    out[...] = total * scale


def tokens_kernel(z, full, turned, out):
    for c in range(z.local):
        part = matmul(turned[c], full[c], 1, 1)
        out[:, c * z.block : (c + 1) * z.block] = part.astype(jnp.bfloat16)


def shaped(kind, *shape):
    return jax.ShapeDtypeStruct(shape, kind)


def run(body, outs, scratch, inputs, products, after=()):
    def skip(*refs):
        body(*refs[: len(inputs)], *refs[len(inputs) + len(after) :])

    specs = [
        pl.BlockSpec(memory_space=pltpu.SMEM if one.dtype == jnp.int32 else pltpu.VMEM) for one in inputs
    ]
    moved = sum(math.prod(one.shape) * one.dtype.itemsize for one in (*inputs, *outs))
    return pl.pallas_call(
        skip,
        out_shape=outs,
        in_specs=specs + [pl.BlockSpec(memory_space=pl.ANY)] * len(after),
        out_specs=[pl.BlockSpec(memory_space=pltpu.VMEM) for _ in outs],
        scratch_shapes=scratch,
        compiler_params=pltpu.CompilerParams(vmem_limit_bytes=vmem_bytes),
        cost_estimate=pl.CostEstimate(flops=CFG["flops"] * products, bytes_accessed=moved, transcendentals=0),
    )(*inputs, *after)


def on_device(tokens, cotangent, right_one, left_one, right_two, left_two):
    z = Sizes(tokens, right_one)
    bf16, f32 = jnp.bfloat16, jnp.float32
    scale = 1.0 / math.sqrt(z.tokens * z.dp)
    ids = jnp.stack([lax.axis_index("dp"), lax.axis_index("mp")]).astype(jnp.int32)
    products = z.local * z.block * z.block * z.tokens
    weight = shaped(bf16, z.local, z.block, z.block)
    acts = shaped(bf16, z.local, z.block, z.tokens)
    sends = [shaped(bf16, z.local * z.local, z.tokens)] * z.mp
    halves = [
        shaped(bf16, z.dp // 2, z.local * z.rows, z.block),
        shaped(f32, z.dp // 2, z.local * z.rows, z.block),
    ]
    mixed = pltpu.VMEM((z.tokens // lane_tile, z.block * z.local, lane_tile), f32)
    sums = pltpu.VMEM((z.local, z.block, z.block), f32)
    held = pltpu.VMEM((z.local, z.block, z.tokens), bf16)

    part = functools.partial
    along = list(reversed(steps_of(z.dp)))
    orders = {name: [*along, 1] if kind == "far" else [1, *along] for name, kind in CFG["scatters"].items()}

    def on(key, *values):
        return values if CFG[key] else ()

    near = CFG["near"]
    first, inner = Pieces(right_one), Joined(left_one, near[0])
    which = dict(outer=None, second=None)
    if CFG["pair"]:
        outer = second = Joined(jnp.stack([left_two, right_two]), near[1])
        which = dict(outer=0, second=1)
    else:
        outer, second = Joined(left_two, near[1]), Joined(right_two, near[2])

    wave0 = first.wave()
    i0 = inner.step()
    turned_up = run(part(turn_kernel, z), sends, [mixed], [ids, cotangent], 0)
    upstream = exchange(turned_up)
    wave1 = first.wave()
    o0 = outer.step() if near[1] else outer.step(*on("A1", *wave0[:1]))
    s0 = [] if CFG["pair"] else second.step(*on("A3", *wave0[:1])) if not near[2] else second.step()
    i1 = inner.step(*on("A2", turned_up[1]), *on("D1", *s0), *on("D2", *o0))
    wave2 = first.wave()
    first_layout, first_pieces = first.finish()
    right_first, *parts = run(
        part(first_kernel, z, first_layout, None),
        [weight] + sends,
        [mixed],
        [ids, tokens, *first_pieces],
        products,
        [*on("A4", *s0), *on("A5", *i1), *on("A6", *o0), *on("A7", *upstream[2:3]), *on("A8", *upstream[3:4]), *on("A9", *upstream[1:2])],
    )
    k1 = parts[1]
    first_columns = exchange(parts)
    i2 = inner.step(*on("B1", *wave2), *on("BC", k1))
    o1 = outer.step(*on("B2", k1), *on("B3", first_columns[1]), *on("BA", first_columns[2]))
    s1 = [] if CFG["pair"] else second.step(*on("B4", k1), *on("B5", first_columns[1]), *on("B8", first_columns[2]), *on("B9", *i2))
    inner_layout, inner_pieces = inner.finish()
    left_first, columns, *parts = run(
        part(middle_kernel, z, inner_layout, None, 0),
        [weight, acts] + sends,
        [mixed],
        [ids, *inner_pieces, *first_columns],
        products,
        [*on("B6", *s1), *on("B7", *o1)],
    )
    k3 = parts[1]
    preact = exchange(parts)
    outer.step(*on("C1", k3), *on("E3", preact[1]))
    [] if CFG["pair"] else second.step(*on("C2", k3), *on("E1", preact[1]), *on("E2", preact[2]))
    outer_layout, outer_pieces = outer.finish()
    second_layout, second_pieces = second.finish()
    _, upstream_columns, *parts = run(
        part(middle_kernel, z, outer_layout, which["outer"], 1),
        [weight, acts] + sends,
        [mixed],
        [ids, *outer_pieces, *upstream],
        products,
        [*on("C3", k3), *on("C4", preact[1]), *on("E4", preact[2])],
    )
    second_rows = exchange(parts)
    right_second, hidden, second_back, *parts = run(
        part(gelu_kernel, z, second_layout, which["second"]),
        [weight, acts, acts] + sends,
        [mixed],
        [ids, *second_pieces, *preact, *second_rows],
        products,
    )
    first_upstream = exchange(parts)
    parts = run(
        part(second_kernel, z),
        sends,
        [mixed],
        [ids, right_second, hidden],
        products,
        [*on("T1", first_upstream[1]), *on("T14", first_upstream[2])],
    )
    second_columns = exchange(parts)
    right_two_halves = run(
        part(grad_kernel, z, orders["second"]),
        halves,
        [sums],
        [ids, hidden, second_back],
        products,
        [*on("T2", first_upstream[1]), *on("T3", second_columns[1]), *on("T15", first_upstream[2])],
    )
    scatter = {"second": Scatter(right_two_halves, orders["second"], CFG["scatters"]["second"] == "direct")}
    scatter["second"].step()
    upstream_rows, *parts = run(
        part(back_kernel, z),
        [acts] + sends,
        [mixed],
        [ids, left_first, *first_upstream],
        products,
        [*on("T4", *right_two_halves[:1]), *on("T16", parts[1])],
    )
    def left_one(after):
        return run(
            part(grad_kernel, z, orders["inner"]), halves, [sums], [ids, columns, upstream_rows], products, after
        )

    if CFG["T5"]:
        left_one_halves = left_one([])
        parts[1] = wait_for(parts[1], left_one_halves[0])
    first_rows = exchange(parts)
    if not CFG["T5"]:
        left_one_halves = left_one([*on("T8", first_rows[1]), *on("T11", first_rows[2])])
    scatter["inner"] = Scatter(left_one_halves, orders["inner"], CFG["scatters"]["inner"] == "direct")
    scatter["inner"].step()
    left_two_halves = run(
        part(placed_grad_kernel, z, orders["outer"]),
        halves,
        [held, sums],
        [ids, upstream_columns, *second_columns],
        products,
        [*on("T6", first_rows[1]), *on("T9", first_rows[2]), *on("T12", first_rows[3])],
    )
    scatter["outer"] = Scatter(left_two_halves, orders["outer"], CFG["scatters"]["outer"] == "direct")
    o_held = scatter["outer"].step()
    totals = {}
    r_pieces = []
    if CFG["S"]:
        r_pieces = scatter["second"].send(*on("T10", first_rows[2]), *on("T13", first_rows[3]))
    else:
        totals["second"] = scatter["second"].finish(*on("T10", first_rows[2]), *on("T13", first_rows[3])) * scale
    turned, *right_one_halves = run(
        part(last_grad_kernel, z, orders["first"]),
        [shaped(bf16, z.local, z.tokens, z.block)] + halves,
        [held, sums],
        [ids, tokens, *first_rows],
        products,
        [*(on("Q1", totals["second"]) if not CFG["S"] else on("Q1", r_pieces[0])), *on("Q2", left_two_halves[0]), *on("Q3", scatter["inner"].held), *on("Q8", scatter["outer"].held)],
    )
    scatter["first"] = Scatter(right_one_halves, orders["first"], CFG["scatters"]["first"] == "direct")
    f_held = scatter["first"].step()
    if CFG["S"]:
        totals["second"] = scatter["second"].collect(scale, *on("S1", f_held))
        scatter["inner"].send()
        scatter["outer"].send(*on("S3", f_held))
        f_pieces = scatter["first"].send()
        totals["inner"] = scatter["inner"].collect(scale, *on("S2", f_held), *on("S4", f_pieces[0]))
        totals["outer"] = scatter["outer"].collect(scale, *on("S5", f_pieces[0]))
        totals["first"] = scatter["first"].collect(scale)
    else:
        totals["inner"] = scatter["inner"].finish() * scale
        totals["first"] = scatter["first"].finish(*on("Q4", totals["inner"]), *on("Q5", o_held)) * scale
        totals["outer"] = scatter["outer"].finish(*on("Q9", f_held)) * scale
    (tokens_grad,) = run(
        part(tokens_kernel, z),
        [shaped(bf16, z.tokens, z.local * z.block)],
        [],
        [right_first, turned],
        products,
        [*on("Q6", f_held), *on("Q7", totals["inner"])],
    )
    summed = [
        totals[name].reshape(z.local, z.rows, z.block) for name in ("first", "inner", "second", "outer")
    ]
    return (tokens_grad, *summed)


def solution(mesh):
    placed = (
        P("dp", "mp"),
        P("dp", "mp"),
        P("mp", "dp", None),
        P("mp", "dp", None),
        P("mp", "dp", None),
        P("mp", "dp", None),
    )
    return jax.shard_map(
        on_device,
        mesh=mesh,
        in_specs=placed,
        out_specs=(
            P("dp", "mp"),
            P("mp", "dp", None),
            P("mp", "dp", None),
            P("mp", "dp", None),
            P("mp", "dp", None),
        ),
        check_vma=False,
    )
```

```python
import functools
import math

import jax
import jax.numpy as jnp
from jax import lax
from jax.experimental import pallas as pl
from jax.experimental.pallas import tpu as pltpu
from jax.sharding import PartitionSpec as P

half_root = 0.7071067811865476
inv_root_tau = 0.3989422804014327
lane_tile = 128
packed_rows = 16
vmem_bytes = 14 * 1024 * 1024


def gelu_parts(values):
    normal_cdf = 0.5 * (1.0 + lax.erf(values * half_root))
    return (
        values * normal_cdf,
        normal_cdf + values * jnp.exp(-0.5 * values * values) * inv_root_tau,
    )


def hop(source, axis, offset):
    size = lax.axis_size(axis)
    return lax.ppermute(source, axis, [(i, i ^ offset) for i in range(size)])


def exchange(sends):
    return [sends[0]] + [hop(sends[q], "mp", q) for q in range(1, len(sends))]


def nothing_kernel(*refs):
    pass


def wait_for(source, *others):
    if not others:
        return source
    return pl.pallas_call(
        nothing_kernel,
        out_shape=shaped(source.dtype, *source.shape),
        in_specs=[pl.BlockSpec(memory_space=pl.ANY)] * (1 + len(others)),
        out_specs=pl.BlockSpec(memory_space=pl.ANY),
        input_output_aliases={0: 0},
        compiler_params=pltpu.CompilerParams(vmem_limit_bytes=vmem_bytes),
    )(source, *others)


def steps_of(size):
    return [1 << bit for bit in reversed(range(1, size.bit_length() - 1))]


class Pieces:
    def __init__(self, shard):
        self.size = lax.axis_size("dp")
        self.depth = 0
        self.whole = None
        self.got = {0: shard[None]}
        if shard.shape[1] % packed_rows:
            self.whole = lax.all_gather(shard, "dp", axis=1, tiled=True)[None]

    def wave(self, *others):
        self.depth += 1
        offsets = [o for o in range(self.size) if o.bit_count() == self.depth]
        if self.whole is not None:
            return []
        for o in offsets:
            low = o & -o
            self.got[o] = hop(wait_for(self.got[o ^ low], *others), "dp", low)
        return [self.got[o] for o in offsets]

    def finish(self):
        if self.whole is not None:
            return ((0,),), (self.whole,)
        while len(self.got) < self.size:
            self.wave()
        return tuple((o,) for o in self.got), tuple(self.got.values())


class Joined:
    def __init__(self, shard, near):
        self.steps = steps_of(lax.axis_size("dp"))
        self.steps.insert(0 if near else len(self.steps), 1)
        self.offsets, self.held = (0,), shard[None]
        self.arrived = None
        if shard.shape[-2] % packed_rows:
            self.steps = []
            self.held = lax.all_gather(shard, "dp", axis=shard.ndim - 2, tiled=True)[None]

    def step(self, *others):
        if not self.steps:
            return []
        if self.arrived is not None:
            self.held = join(self.held, self.arrived, others)
            self.offsets += self.new
            others = ()
        step = self.steps.pop(0)
        self.new = tuple(o ^ step for o in self.offsets)
        self.arrived = hop(wait_for(self.held, *others), "dp", step)
        return [self.arrived]

    def finish(self):
        while self.steps:
            self.step()
        if self.arrived is None:
            return ((0,),), (self.held,)
        return (self.offsets, self.new), (self.held, self.arrived)


class Scatter:
    def __init__(self, halves, steps):
        self.sent, self.kept = halves
        self.steps = steps

    def step(self):
        self.held = self.kept + hop(self.sent, "dp", self.steps[0]).astype(jnp.float32)

    def finish(self):
        bits = list(reversed(self.steps[1:]))
        total = self.held[0]
        for q in range(1, self.held.shape[0]):
            offset = sum(bit for k, bit in enumerate(bits) if q >> k & 1)
            total = total + hop(self.held[q].astype(jnp.bfloat16), "dp", offset).astype(jnp.float32)
        return total


def join_kernel(one, two, out):
    out[: one.shape[0]] = one[...]
    out[one.shape[0] :] = two[...]


def join(one, two, after):
    count = one.shape[0] + two.shape[0]
    (out,) = run(join_kernel, [shaped(one.dtype, count, *one.shape[1:])], [], [one, two], 0, after)
    return out


class Sizes:
    def __init__(self, tokens, right_one):
        self.tokens = tokens.shape[0]
        self.local, self.rows, self.block = right_one.shape
        self.dp = lax.axis_size("dp")
        self.mp = lax.axis_size("mp")


def matmul(left, right, left_dim, right_dim):
    return lax.dot_general(
        left, right, (((left_dim,), (right_dim,)), ((), ())), preferred_element_type=jnp.float32
    )


def place(full, pieces, layout, me):
    local, block, width = full.shape
    rows = block // sum(len(offsets) for offsets in layout)
    for piece, offsets in zip(pieces, layout, strict=True):
        for k, offset in enumerate(offsets):
            start = 0 if rows == block else pl.multiple_of((me ^ offset) * rows, rows)
            full[:, pl.ds(start, rows), :] = piece[k].reshape(local, rows, width)


def place_arrived(full, pieces, me):
    local, block, width = full.shape
    rows = block // len(pieces)
    for q, piece in enumerate(pieces):
        start = pl.multiple_of((me ^ q) * rows, rows)
        full[:, pl.ds(start, rows), :] = piece[...].reshape(local, rows, width)


def spread(mixed, sends, index):
    size = sends[0].shape[0]
    for q, send in enumerate(sends):
        start = pl.multiple_of((index ^ q) * size, size)
        for h in range(mixed.shape[0]):
            lanes = slice(h * lane_tile, (h + 1) * lane_tile)
            send[:, lanes] = mixed[h, pl.ds(start, size), :].astype(jnp.bfloat16)


def split_grad(sums, sent, kept, index, steps):
    local, block, width = sums.shape
    offsets = [0]
    for step in reversed(steps[1:]):
        offsets += [offset ^ step for offset in offsets]
    rows = block // (2 * len(offsets))
    for q, offset in enumerate(offsets):
        for target, number in ((kept, offset), (sent, offset ^ steps[0])):
            start = pl.multiple_of((index ^ number) * rows, rows)
            part = sums[:, pl.ds(start, rows), :].reshape(local * rows, width)
            target[q] = part.astype(target.dtype)


def column(mixed, c, local, value):
    for h in range(mixed.shape[0]):
        lanes = slice(h * lane_tile, (h + 1) * lane_tile)
        mixed[h, pl.ds(c, value.shape[0], stride=local), :] = value[:, lanes]


def turn_kernel(z, ids, cotangent, *refs):
    sends, (mixed,) = refs[: z.mp], refs[z.mp :]
    for c in range(z.local):
        part = cotangent[:, c * z.block : (c + 1) * z.block].astype(jnp.float32)
        column(mixed, c, z.local, part.T)
    spread(mixed, sends, ids[1])


def first_kernel(z, layout, ids, tokens, *refs):
    pieces, refs = refs[: len(layout)], refs[len(layout) :]
    full, sends, mixed = refs[0], refs[1 : 1 + z.mp], refs[1 + z.mp]
    place(full, pieces, layout, ids[0])
    for c in range(z.local):
        part = tokens[:, c * z.block : (c + 1) * z.block]
        column(mixed, c, z.local, matmul(full[c], part, 0, 1))
    spread(mixed, sends, ids[1])


def middle_kernel(z, layout, side, ids, *refs):
    pieces, refs = refs[: len(layout)], refs[len(layout) :]
    arrived, refs = refs[: z.mp], refs[z.mp :]
    full, columns, sends, mixed = refs[0], refs[1], refs[2 : 2 + z.mp], refs[2 + z.mp]
    place(full, pieces, layout, ids[0])
    place_arrived(columns, arrived, ids[1])
    for c in range(z.local):
        column(mixed, c, z.local, matmul(full[c], columns[c], side, 0))
    spread(mixed, sends, ids[1])


def back_kernel(z, ids, full, *refs):
    arrived, refs = refs[: z.mp], refs[z.mp :]
    columns, sends, mixed = refs[0], refs[1 : 1 + z.mp], refs[1 + z.mp]
    place_arrived(columns, arrived, ids[1])
    for c in range(z.local):
        column(mixed, c, z.local, matmul(full[c], columns[c], 1, 0))
    spread(mixed, sends, ids[1])


def gelu_kernel(z, layout, ids, *refs):
    pieces, refs = refs[: len(layout)], refs[len(layout) :]
    preact, backs, refs = refs[: z.mp], refs[z.mp : 2 * z.mp], refs[2 * z.mp :]
    full, hidden, back, sends, mixed = refs[0], refs[1], refs[2], refs[3 : 3 + z.mp], refs[3 + z.mp]
    place(full, pieces, layout, ids[0])
    place_arrived(hidden, preact, ids[1])
    place_arrived(back, backs, ids[1])
    for c in range(z.local):
        activated, slope = gelu_parts(hidden[c].astype(jnp.float32))
        hidden[c] = activated.astype(jnp.bfloat16)
        column(mixed, c, z.local, matmul(full[c], back[c], 1, 0) * slope)
    spread(mixed, sends, ids[1])


def second_kernel(z, ids, full, hidden, *refs):
    sends, (mixed,) = refs[: z.mp], refs[z.mp :]
    for c in range(z.local):
        column(mixed, c, z.local, matmul(full[c], hidden[c], 0, 0))
    spread(mixed, sends, ids[1])


def grad_kernel(z, steps, ids, left, right, sent, kept, sums):
    for c in range(z.local):
        sums[c] = matmul(left[c], right[c], 1, 1)
    split_grad(sums, sent, kept, ids[0], steps)


def placed_grad_kernel(z, steps, ids, right, *refs):
    pieces, (sent, kept, left, sums) = refs[: z.mp], refs[z.mp :]
    place_arrived(left, pieces, ids[1])
    grad_kernel(z, steps, ids, left, right, sent, kept, sums)


def last_grad_kernel(z, steps, ids, tokens, *refs):
    pieces, (turned, sent, kept, back, sums) = refs[: z.mp], refs[z.mp :]
    place_arrived(back, pieces, ids[1])
    for c in range(z.local):
        block = back[c].T
        turned[c] = block
        sums[c] = matmul(tokens[:, c * z.block : (c + 1) * z.block], block, 0, 0)
    split_grad(sums, sent, kept, ids[0], steps)


def tokens_kernel(z, full, turned, out):
    for c in range(z.local):
        part = matmul(turned[c], full[c], 1, 1)
        out[:, c * z.block : (c + 1) * z.block] = part.astype(jnp.bfloat16)


def shaped(kind, *shape):
    return jax.ShapeDtypeStruct(shape, kind)


def run(body, outs, scratch, inputs, products, after=()):
    def skip(*refs):
        body(*refs[: len(inputs)], *refs[len(inputs) + len(after) :])

    specs = [
        pl.BlockSpec(memory_space=pltpu.SMEM if one.dtype == jnp.int32 else pltpu.VMEM) for one in inputs
    ]
    moved = sum(math.prod(one.shape) * one.dtype.itemsize for one in (*inputs, *outs))
    return pl.pallas_call(
        skip,
        out_shape=outs,
        in_specs=specs + [pl.BlockSpec(memory_space=pl.ANY)] * len(after),
        out_specs=[pl.BlockSpec(memory_space=pltpu.VMEM) for _ in outs],
        scratch_shapes=scratch,
        compiler_params=pltpu.CompilerParams(vmem_limit_bytes=vmem_bytes),
        cost_estimate=pl.CostEstimate(flops=2 * products, bytes_accessed=moved, transcendentals=0),
    )(*inputs, *after)


def on_device(tokens, cotangent, right_one, left_one, right_two, left_two):
    z = Sizes(tokens, right_one)
    bf16, f32 = jnp.bfloat16, jnp.float32
    scale = 1.0 / math.sqrt(z.tokens * z.dp)
    ids = jnp.stack([lax.axis_index("dp"), lax.axis_index("mp")]).astype(jnp.int32)
    products = z.local * z.block * z.block * z.tokens
    weight = shaped(bf16, z.local, z.block, z.block)
    acts = shaped(bf16, z.local, z.block, z.tokens)
    sends = [shaped(bf16, z.local * z.local, z.tokens)] * z.mp
    halves = [
        shaped(bf16, z.dp // 2, z.local * z.rows, z.block),
        shaped(f32, z.dp // 2, z.local * z.rows, z.block),
    ]
    mixed = pltpu.VMEM((z.tokens // lane_tile, z.block * z.local, lane_tile), f32)
    sums = pltpu.VMEM((z.local, z.block, z.block), f32)
    held = pltpu.VMEM((z.local, z.block, z.tokens), bf16)

    part = functools.partial
    orders = [1, *reversed(steps_of(z.dp))]

    first, inner = Pieces(right_one), Joined(left_one, near=True)
    outer, second = Joined(left_two, near=True), Joined(right_two, near=False)

    first.wave()
    inner.step()
    turned_up = run(part(turn_kernel, z), sends, [mixed], [ids, cotangent], 0)
    upstream = exchange(turned_up)
    first.wave()
    outer.step()
    second.step()
    inner.step()
    first.wave()
    first_layout, first_pieces = first.finish()
    right_first, *parts = run(
        part(first_kernel, z, first_layout),
        [weight] + sends,
        [mixed],
        [ids, tokens, *first_pieces],
        products,
        [*upstream[2:3]],
    )
    first_columns = exchange(parts)
    inner.step()
    outer.step()
    second.step()
    inner_layout, inner_pieces = inner.finish()
    left_first, columns, *parts = run(
        part(middle_kernel, z, inner_layout, 0),
        [weight, acts] + sends,
        [mixed],
        [ids, *inner_pieces, *first_columns],
        products,
    )
    preact = exchange(parts)
    outer.step()
    second.step()
    outer_layout, outer_pieces = outer.finish()
    second_layout, second_pieces = second.finish()
    _, upstream_columns, *parts = run(
        part(middle_kernel, z, outer_layout, 1),
        [weight, acts] + sends,
        [mixed],
        [ids, *outer_pieces, *upstream],
        products,
    )
    second_rows = exchange(parts)
    right_second, hidden, second_back, *parts = run(
        part(gelu_kernel, z, second_layout),
        [weight, acts, acts] + sends,
        [mixed],
        [ids, *second_pieces, *preact, *second_rows],
        products,
    )
    first_upstream = exchange(parts)
    parts = run(
        part(second_kernel, z),
        sends,
        [mixed],
        [ids, right_second, hidden],
        products,
    )
    second_columns = exchange(parts)
    right_two_halves = run(
        part(grad_kernel, z, orders),
        halves,
        [sums],
        [ids, hidden, second_back],
        products,
    )
    scatter = {"second": Scatter(right_two_halves, orders)}
    scatter["second"].step()
    upstream_rows, *parts = run(
        part(back_kernel, z),
        [acts] + sends,
        [mixed],
        [ids, left_first, *first_upstream],
        products,
    )
    left_one_halves = run(part(grad_kernel, z, orders), halves, [sums], [ids, columns, upstream_rows], products)
    parts[1] = wait_for(parts[1], left_one_halves[0])
    first_rows = exchange(parts)
    scatter["inner"] = Scatter(left_one_halves, orders)
    scatter["inner"].step()
    left_two_halves = run(
        part(placed_grad_kernel, z, orders),
        halves,
        [held, sums],
        [ids, upstream_columns, *second_columns],
        products,
    )
    scatter["outer"] = Scatter(left_two_halves, orders)
    scatter["outer"].step()
    totals = {"second": scatter["second"].finish() * scale}
    turned, *right_one_halves = run(
        part(last_grad_kernel, z, orders),
        [shaped(bf16, z.local, z.tokens, z.block)] + halves,
        [held, sums],
        [ids, tokens, *first_rows],
        products,
        [scatter["inner"].held],
    )
    scatter["first"] = Scatter(right_one_halves, orders)
    scatter["first"].step()
    totals["inner"] = scatter["inner"].finish() * scale
    totals["first"] = scatter["first"].finish() * scale
    totals["outer"] = scatter["outer"].finish() * scale
    (tokens_grad,) = run(
        part(tokens_kernel, z),
        [shaped(bf16, z.tokens, z.local * z.block)],
        [],
        [right_first, turned],
        products,
    )
    summed = [
        totals[name].reshape(z.local, z.rows, z.block) for name in ("first", "inner", "second", "outer")
    ]
    return (tokens_grad, *summed)


def solution(mesh):
    placed = (
        P("dp", "mp"),
        P("dp", "mp"),
        P("mp", "dp", None),
        P("mp", "dp", None),
        P("mp", "dp", None),
        P("mp", "dp", None),
    )
    return jax.shard_map(
        on_device,
        mesh=mesh,
        in_specs=placed,
        out_specs=(
            P("dp", "mp"),
            P("mp", "dp", None),
            P("mp", "dp", None),
            P("mp", "dp", None),
            P("mp", "dp", None),
        ),
        check_vma=False,
    )
```
